32 devices in a mesh: batch: 2 (over x), seq: 8 (over z, y), mp: 2 (over core).
Axes of the slice: x: 2, y: 2, z: 4, core: 2. Of those that a mesh axis runs over, the one named last changes fastest.
Arguments:
- tokens: bfloat16 [8192, 2048], P(('batch', 'seq'), 'mp'), parts along dimension 0, may hold values from -36 to 36
- modulation: float32 [12, 2048], P('batch'), parts along dimension 0, may hold values from -3 to 3
- query_weight: bfloat16 [2048, 1024], P(None, 'mp'), may hold values from -0.125 to 0.125
- key_weight: bfloat16 [2048, 1024], P(None, 'mp'), may hold values from -0.125 to 0.125
- value_weight: bfloat16 [2048, 1024], P(None, 'mp'), may hold values from -0.125 to 0.125
- out_weight: bfloat16 [1024, 2048], P('mp'), may hold values from -0.1875 to 0.1875
- query_gain: float32 [128], replicated, may hold values from 1 to 2
- key_gain: float32 [128], replicated, may hold values from 1 to 2
- conv_weight: bfloat16 [27, 2048], P(None, 'mp'), may hold values from -1.25 to 1.25
Outputs:
- mixed: bfloat16 [8192, 2048], P(('batch', 'seq'), 'mp'), parts along dimension 0
The draws below stay inside these ranges and needn't reach their ends.
There are 2 independent parts, one for each index of `batch`. The reference program is written for one: setup_inputs(seed, part) draws one part's arguments, and reference() takes and returns one part's arrays. A program takes and returns all parts, laid end to end along the dimension named above; an argument that names none is the same for every part. Nothing has to cross between parts.
All inputs are finite; a program needn't handle non-finite values.
Results may differ from the reference program's by a relative error of at most 0.0065.
Values may be sent and summed in bfloat16 or wider, within the bound.
A program may use at most 64 MiB of HBM per device.

```python
import math
import jax
import jax.numpy as jnp
from jax import lax

D = 2048
HEADS = 8
HD = 128
GY = 8
GX = 16
ZDEV = 4
INNER = 1024
PLANE = 128
TOKENS = 4096
RADIUS = 8


def draw_tokens(key, part):
    key_cols, key_rows, key_noise = jax.random.split(jax.random.fold_in(key, 17), 3)
    col_factor = jnp.exp(jax.random.uniform(key_cols, (1, D), jnp.float32, math.log(0.6), math.log(1.5)))
    col_pos = jnp.arange(D, dtype=jnp.float32)[None, :] / D
    row_scale = jnp.exp(jax.random.uniform(key_rows, (TOKENS, 1), jnp.float32, math.log(0.3), math.log(2.0)))
    col_scale = 0.5 * jnp.exp(col_pos * math.log(5.0)) * col_factor
    noise_vals = jnp.clip(jax.random.normal(key_noise, (TOKENS, D), jnp.float32), -4.0, 4.0)
    result_vals = noise_vals * row_scale * col_scale
    return result_vals.astype(jnp.bfloat16)


def level_of(rng, extent, cuts, smallest, top_value):
    factor_of = 1.0
    for position, blocks in cuts:
        heights = jax.random.uniform(jax.random.fold_in(jax.random.fold_in(rng, 6), position), (blocks,), jnp.float32, smallest / len(cuts), top_value / len(cuts))
        factor_of = factor_of * jnp.repeat(jnp.exp(heights), extent[position] // blocks).reshape((-1,) + (1,) * (len(extent) - 1 - position))
    return factor_of


def gaussian(key, dims, scale, limit, shards=(), kind=jnp.bfloat16):
    entries = scale * jax.random.normal(key, dims, jnp.float32)
    if shards:
        entries = entries * level_of(key, dims, shards, -0.22, 0.18)
    return jnp.clip(entries, -limit, limit).astype(kind)


def setup_inputs(seed: int = 0, part: int = 0) -> dict:
    key_of = jax.random.split(jax.random.key(seed), 10)
    part_keys = jax.random.split(jax.random.fold_in(key_of[9], part), 10)
    return {
        "tokens": draw_tokens(jax.random.fold_in(jax.random.fold_in(key_of[9], part), 71), part),
        "modulation": gaussian(part_keys[1], (6, D), 0.5, 3.0, (), jnp.float32),
        "query_weight": gaussian(key_of[2], (D, INNER), D ** -0.5, 0.125, ((1, 2),)),
        "key_weight": gaussian(key_of[3], (D, INNER), D ** -0.5, 0.125, ((1, 2),)),
        "value_weight": gaussian(key_of[4], (D, INNER), D ** -0.5, 0.125, ((1, 2),)),
        "out_weight": gaussian(key_of[5], (INNER, D), INNER ** -0.5, 0.1875, ((0, 2),)),
        "query_gain": jnp.clip(jax.random.uniform(key_of[6], (HD,), jnp.float32, 1.0, 2.0), 1.0, 2.0),
        "key_gain": jnp.clip(jax.random.uniform(key_of[7], (HD,), jnp.float32, 1.0, 2.0), 1.0, 2.0),
        "conv_weight": gaussian(key_of[8], (27, D), 27 ** -0.5, 1.25, ((1, 2),)),
    }


EPS = 1e-06

def layer_norm(values):
    row_mean = lax.optimization_barrier(jnp.mean(values, axis=-1, keepdims=True))
    row_square = lax.optimization_barrier(jnp.mean(values * values, axis=-1, keepdims=True))
    variance = row_square - row_mean * row_mean
    return (values - row_mean) * lax.rsqrt(variance + EPS)

def head_norm(values, gain_vec):
    mean_sq = lax.optimization_barrier(jnp.mean(values * values, axis=-1, keepdims=True))
    return values * lax.rsqrt(mean_sq + EPS) * gain_vec

def reference(tokens, modulation, query_weight, key_weight, value_weight, out_weight, query_gain, key_gain, conv_weight):
    full_vals = tokens.astype(jnp.float32)
    normed = (layer_norm(full_vals) * (1.0 + modulation[1]) + modulation[0]).astype(jnp.bfloat16)
    queries = jnp.dot(normed, query_weight, preferred_element_type=jnp.float32).reshape(TOKENS, HEADS, HD)
    queries = (head_norm(queries, query_gain) * HD ** (-0.5)).astype(jnp.bfloat16)
    key_vals = jnp.dot(normed, key_weight, preferred_element_type=jnp.float32).reshape(TOKENS, HEADS, HD)
    key_vals = head_norm(key_vals, key_gain).astype(jnp.bfloat16)
    value_vals = jnp.dot(normed, value_weight, preferred_element_type=jnp.float32).astype(jnp.bfloat16)
    value_vals = value_vals.reshape(TOKENS, HEADS, HD)
    plane_count = TOKENS // PLANE
    q_planes = queries.reshape(plane_count, PLANE, HEADS, HD)
    k_planes = key_vals.reshape(plane_count, PLANE, HEADS, HD)
    v_planes = value_vals.reshape(plane_count, PLANE, HEADS, HD)
    k_wrapped = jnp.concatenate([k_planes[plane_count - RADIUS:], k_planes, k_planes[:RADIUS]], axis=0)
    v_wrapped = jnp.concatenate([v_planes[plane_count - RADIUS:], v_planes, v_planes[:RADIUS]], axis=0)
    span_planes = ZDEV + 2 * RADIUS

    def one_block(block_idx):
        start = (block_idx * ZDEV).astype(jnp.int32)
        q_blk = lax.dynamic_slice_in_dim(q_planes, start, ZDEV, 0).reshape(ZDEV * PLANE, HEADS, HD).astype(jnp.float32)
        k_blk = lax.dynamic_slice_in_dim(k_wrapped, start, span_planes, 0).reshape(span_planes * PLANE, HEADS, HD).astype(jnp.float32)
        v_blk = lax.dynamic_slice_in_dim(v_wrapped, start, span_planes, 0).reshape(span_planes * PLANE, HEADS, HD).astype(jnp.float32)
        scores = jnp.einsum('qhd,khd->hqk', q_blk, k_blk)
        q_plane = jnp.arange(ZDEV * PLANE, dtype=jnp.int32) // PLANE
        k_plane = jnp.arange(span_planes * PLANE, dtype=jnp.int32) // PLANE - RADIUS
        inside = jnp.abs(q_plane[:, None] - k_plane[None, :]) <= RADIUS
        weights = jnp.where(inside[None], jnp.exp(scores), jnp.float32(0.0))
        denom = lax.optimization_barrier(jnp.sum(weights, axis=-1))
        rounded = lax.optimization_barrier(weights.astype(jnp.bfloat16))
        summed = jnp.einsum('hqk,khd->qhd', rounded.astype(jnp.float32), v_blk)
        return (summed / jnp.transpose(denom)[:, :, None]).astype(jnp.bfloat16)
    attn_out = lax.map(one_block, jnp.arange(plane_count // ZDEV, dtype=jnp.int32)).reshape(TOKENS, HEADS * HD)
    attended = jnp.dot(attn_out, out_weight, preferred_element_type=jnp.float32)
    residual = full_vals + modulation[2] * attended
    shaped = (layer_norm(residual) * (1.0 + modulation[4]) + modulation[3]).astype(jnp.bfloat16)
    grid_vals = shaped.reshape(plane_count, GY, GX, D)
    wrapped = jnp.concatenate([grid_vals[plane_count - 1:], grid_vals, grid_vals[:1]], axis=0)
    padded = jnp.pad(wrapped, ((0, 0), (1, 1), (1, 1), (0, 0)))
    conv_taps = conv_weight.astype(jnp.float32)
    conv_sum = jnp.zeros((plane_count, GY, GX, D), jnp.float32)
    for dz_off in range(3):
        for dy_off in range(3):
            for dx_off in range(3):
                window = padded[dz_off:dz_off + plane_count, dy_off:dy_off + GY, dx_off:dx_off + GX]
                conv_sum = conv_sum + window * conv_taps[(dz_off * 3 + dy_off) * 3 + dx_off]
    mixed = residual + modulation[5] * jax.nn.gelu(conv_sum.reshape(TOKENS, D))
    return mixed.astype(jnp.bfloat16)
```

```python
import functools
import math

import jax
import jax.numpy as jnp
from jax import lax
from jax.experimental import pallas as pl
from jax.experimental.pallas import tpu as pltpu
from jax.sharding import PartitionSpec as P

HD = 128
GX = 16
PLANE = 128
RADIUS = 8
ZDEV = 4
EPS = 1e-06
MESH = pl.DeviceIdType.MESH
F32 = jnp.float32
BF16 = jnp.bfloat16

OWN, PAIR, BELOW, ABOVE, PASSED = range(5)


def block_kernel(
    n,
    x_ref,
    mod_ref,
    qg_ref,
    kg_ref,
    cw_ref,
    wq_hbm,
    wk_hbm,
    wv_hbm,
    wo_hbm,
    out_ref,
    wq,
    wk,
    wv,
    wo,
    x_other,
    normed,
    kv,
    qbuf,
    acc,
    den,
    attn,
    part_send,
    part_recv,
    part_own,
    stat_send,
    stat_recv,
    resid,
    pad,
    halo_send,
    halo_recv,
    taps,
    w_sem,
    x_sem,
    kv_send,
    kv_recv,
    part_sem,
    stat_sem,
    halo_ss,
    halo_rs,
):
    toks, half = x_ref.shape
    width = 2 * half
    heads = qbuf.shape[0]
    b = lax.axis_index("batch")
    s = lax.axis_index("seq")
    m = lax.axis_index("mp")
    odd = lax.rem(s, 2)
    pair = s + 1 - 2 * odd
    up1, down1 = lax.rem(s + 1, n), lax.rem(s + n - 1, n)
    up2, down2 = lax.rem(s + 2, n), lax.rem(s + n - 2, n)
    here = pl.multiple_of(m * half, half)
    there = pl.multiple_of((1 - m) * half, half)

    loads = []
    for i, (src, dst) in enumerate(((wk_hbm, wk), (wv_hbm, wv), (wq_hbm, wq), (wo_hbm, wo))):
        load = pltpu.make_async_copy(src, dst, w_sem.at[i])
        load.start()
        loads.append(load)

    peers = [(b, s, 1 - m), (b, up1, m), (b, down1, m), (b, up2, m), (b, down2, m)]
    barrier = pltpu.get_barrier_semaphore()
    for peer in peers:
        pl.semaphore_signal(barrier, inc=1, device_id=peer, device_id_type=MESH)
    pl.semaphore_wait(barrier, len(peers))

    def to(peer, src, dst, send_sem, recv_sem):
        return pltpu.make_async_remote_copy(
            src_ref=src,
            dst_ref=dst,
            send_sem=send_sem,
            recv_sem=recv_sem,
            device_id=peer,
            device_id_type=MESH,
        )

    core = (b, s, 1 - m)
    x_copy = to(core, x_ref, x_other, x_sem.at[0], x_sem.at[1])
    x_copy.start()

    pad[:, 0:GX, :] = jnp.zeros((ZDEV + 2, GX, half), F32)
    pad[:, GX + PLANE :, :] = jnp.zeros((ZDEV + 2, GX, half), F32)
    taps[...] = cw_ref[...].astype(F32)
    acc[...] = jnp.zeros_like(acc)
    den[...] = jnp.zeros_like(den)
    x_copy.wait()

    rows_n = 64

    @pl.loop(0, toks // rows_n)
    def _(i):
        rows = pl.ds(pl.multiple_of(i * rows_n, rows_n), rows_n)
        mine = x_ref[rows, :].astype(F32)
        other = x_other[rows, :].astype(F32)
        total = jnp.sum(mine, axis=-1, keepdims=True) + jnp.sum(other, axis=-1, keepdims=True)
        square = jnp.sum(mine * mine, axis=-1, keepdims=True) + jnp.sum(
            other * other, axis=-1, keepdims=True
        )
        mean = total / width
        inv = lax.rsqrt(square / width - mean * mean + EPS)
        for vals, cols in ((mine, pl.ds(here, half)), (other, pl.ds(there, half))):
            normed[rows, cols] = (
                (vals - mean) * inv * (1.0 + mod_ref[1:2, cols]) + mod_ref[0:1, cols]
            ).astype(BF16)

    fwd_slot = ABOVE - odd
    back_slot = BELOW + odd
    fwd_dst = lax.rem(s + n - 2 + 4 * odd, n)
    back_dst = lax.rem(s + 2 + n - 4 * odd, n)

    def send_fwd(h):
        return to((b, fwd_dst, m), kv.at[OWN, h], kv.at[fwd_slot, h], kv_send.at[0, h], kv_recv.at[0, h])

    def send_pair(h):
        return to((b, pair, m), kv.at[OWN, h], kv.at[PAIR, h], kv_send.at[1, h], kv_recv.at[1, h])

    def send_back(h):
        return to((b, back_dst, m), kv.at[OWN, h], kv.at[back_slot, h], kv_send.at[2, h], kv_recv.at[2, h])

    def send_on(h):
        return to((b, pair, m), kv.at[fwd_slot, h], kv.at[PASSED, h], kv_send.at[3, h], kv_recv.at[3, h])

    def head_norm(vals, gain):
        mean_sq = jnp.mean(vals * vals, axis=-1, keepdims=True)
        return vals * lax.rsqrt(mean_sq + EPS) * gain

    loads[0].wait()
    loads[1].wait()

    @pl.loop(0, heads // 2)
    def _(j):
        cols = pl.ds(pl.multiple_of(j * 2 * HD, 2 * HD), 2 * HD)
        keys = jnp.dot(normed[...], wk[:, cols], preferred_element_type=F32)
        for e in range(2):
            kv[OWN, 2 * j + e, :, 0:HD] = head_norm(
                keys[:, e * HD : (e + 1) * HD], kg_ref[...]
            ).astype(BF16)
        values = jnp.dot(normed[...], wv[:, cols], preferred_element_type=F32)
        for e in range(2):
            kv[OWN, 2 * j + e, :, HD:] = values[:, e * HD : (e + 1) * HD].astype(BF16)
        for e in range(2):
            send_fwd(2 * j + e).start()
            send_pair(2 * j + e).start()

    @pl.loop(0, heads)
    def _(h):
        send_back(h).start()

    loads[2].wait()

    @pl.loop(0, heads // 2)
    def _(j):
        cols = pl.ds(pl.multiple_of(j * 2 * HD, 2 * HD), 2 * HD)
        queries = jnp.dot(normed[...], wq[:, cols], preferred_element_type=F32)
        for e in range(2):
            qbuf[2 * j + e] = (
                head_norm(queries[:, e * HD : (e + 1) * HD], qg_ref[...]) * HD ** (-0.5)
            ).astype(BF16)

    rows_q = 256

    def attend(slot, h, sign):
        keys = kv[slot, h, :, 0:HD]
        values = kv[slot, h, :, HD:]
        for r in range(toks // rows_q):
            rows = pl.ds(r * rows_q, rows_q)
            scores = lax.dot_general(
                qbuf[h, rows, :], keys, (((1,), (1,)), ((), ())), preferred_element_type=F32
            )
            weights = jnp.exp(scores)
            if sign is not None:
                q_plane = (lax.broadcasted_iota(jnp.int32, scores.shape, 0) + r * rows_q) // PLANE
                k_plane = lax.broadcasted_iota(jnp.int32, scores.shape, 1) // PLANE
                gap = 2 * ZDEV + (k_plane - q_plane) * sign
                weights = jnp.where(gap <= RADIUS, weights, 0.0)
            total = weights[:, 0:HD]
            for c in range(1, toks // HD):
                total = total + weights[:, c * HD : (c + 1) * HD]
            den[h, rows, :] += total
            acc[h, rows, :] += jnp.dot(weights.astype(BF16), values, preferred_element_type=F32)

    @pl.loop(0, heads)
    def _(h):
        attend(OWN, h, None)

    @pl.loop(0, heads)
    def _(h):
        send_fwd(h).wait_recv()
        send_on(h).start()
        send_pair(h).wait_recv()
        attend(PAIR, h, None)
        attend(fwd_slot, h, 1 - 2 * odd)

    @pl.loop(0, heads)
    def _(h):
        send_back(h).wait_recv()
        attend(back_slot, h, 2 * odd - 1)

    planes_of = ((0, ZDEV - 1), (1, 2))

    @pl.loop(0, heads)
    def _(h):
        send_on(h).wait_recv()
        attend(PASSED, h, None)
        cols = pl.ds(pl.multiple_of(h * HD, HD), HD)
        for p, planes in enumerate(planes_of):
            for e, plane in enumerate(planes):
                rows = pl.ds(plane * PLANE, PLANE)
                total = jnp.sum(den[h, rows, :], axis=-1, keepdims=True)
                attn[p, e * PLANE : (e + 1) * PLANE, cols] = (acc[h, rows, :] / total).astype(BF16)

    loads[3].wait()
    tile = 256

    def part_copy(p):
        return to(core, part_send.at[p], part_recv.at[p], part_sem.at[0, p], part_sem.at[1, p])

    def stat_copy(p):
        return to(core, stat_send.at[p], stat_recv.at[p], stat_sem.at[0, p], stat_sem.at[1, p])

    for p in range(2):

        @pl.loop(0, half // tile)
        def _(c):
            at = pl.multiple_of(c * tile, tile)
            src = pl.ds(pl.multiple_of(there + at, tile), tile)
            part_send[p, :, pl.ds(at, tile)] = jnp.dot(
                attn[p], wo[:, src], preferred_element_type=F32
            ).astype(BF16)

        part_copy(p).start()

    for p in range(2):

        @pl.loop(0, half // tile)
        def _(c):
            at = pl.multiple_of(c * tile, tile)
            src = pl.ds(pl.multiple_of(here + at, tile), tile)
            part_own[p, :, pl.ds(at, tile)] = jnp.dot(attn[p], wo[:, src], preferred_element_type=F32)

    mine = pl.ds(here, half)
    step = 32
    for p, planes in enumerate(planes_of):
        part_copy(p).wait_recv()
        for e, plane in enumerate(planes):

            @pl.loop(0, PLANE // step)
            def _(i):
                at = pl.multiple_of(i * step, step)
                local = pl.ds(pl.multiple_of(e * PLANE + at, step), step)
                attended = part_own[p, local, :] + part_recv[p, local, :].astype(F32)
                vals = (
                    x_ref[pl.ds(pl.multiple_of(plane * PLANE + at, step), step), :].astype(F32)
                    + mod_ref[2:3, mine] * attended
                )
                resid[plane, pl.ds(at, step), :] = vals
                lane = lax.broadcasted_iota(jnp.int32, (step, HD), 1)
                stat_send[p, local, :] = jnp.where(
                    lane < HD // 2,
                    jnp.sum(vals, axis=-1, keepdims=True),
                    jnp.sum(vals * vals, axis=-1, keepdims=True),
                )

        stat_copy(p).start()

    def halo_up():
        return to((b, up1, m), halo_send.at[1], halo_recv.at[0], halo_ss.at[0], halo_rs.at[0])

    def halo_down():
        return to((b, down1, m), halo_send.at[0], halo_recv.at[1], halo_ss.at[1], halo_rs.at[1])

    for p, planes in enumerate(planes_of):
        stat_copy(p).wait_recv()
        for e, plane in enumerate(planes):

            @pl.loop(0, PLANE // step)
            def _(i):
                at = pl.multiple_of(i * step, step)
                local = pl.ds(pl.multiple_of(e * PLANE + at, step), step)
                stats = stat_send[p, local, :] + stat_recv[p, local, :]
                center = stats[:, 0:1] / width
                spread = stats[:, HD // 2 : HD // 2 + 1] / width - center * center
                shaped = (
                    (resid[plane, pl.ds(at, step), :] - center)
                    * lax.rsqrt(spread + EPS)
                    * (1.0 + mod_ref[4:5, mine])
                    + mod_ref[3:4, mine]
                ).astype(BF16)
                pad[plane + 1, pl.ds(pl.multiple_of(GX + at, GX), step), :] = shaped.astype(F32)
                if p == 0:
                    halo_send[e, pl.ds(at, step), :] = shaped

        if p == 0:
            halo_up().start()
            halo_down().start()

    rows_c = 64

    def convolve(plane, lc):
        lane_at = pl.multiple_of(lc * HD, HD)
        lanes = pl.ds(lane_at, HD)
        gate = mod_ref[5:6, pl.ds(pl.multiple_of(here + lane_at, HD), HD)]
        col = lax.rem(lax.broadcasted_iota(jnp.int32, (rows_c, HD), 0), GX)
        for r in range(PLANE // rows_c):
            sums = [None] * 3
            for dz in range(3):
                for dy in range(3):
                    window = pad[plane + dz, pl.ds(r * rows_c + GX * dy, rows_c), lanes]
                    for dx in range(3):
                        k = (dz * 3 + dy) * 3 + dx
                        term = window * taps[k : k + 1, lanes]
                        sums[dx] = term if sums[dx] is None else sums[dx] + term
            v = (
                sums[1]
                + jnp.where(col > 0, pltpu.roll(sums[0], 1, 0), 0.0)
                + jnp.where(col < GX - 1, pltpu.roll(sums[2], rows_c - 1, 0), 0.0)
            )
            gelu = 0.5 * v * (1.0 + jnp.tanh(math.sqrt(2.0 / math.pi) * (v + 0.044715 * (v * v * v))))
            result = resid[plane, pl.ds(r * rows_c, rows_c), lanes] + gate * gelu
            at = pl.multiple_of(plane * PLANE + r * rows_c, rows_c)
            out_ref[pl.ds(at, rows_c), lanes] = result.astype(BF16)

    chunks = half // HD

    @pl.loop(0, 2 * chunks)
    def _(i):
        convolve(1 + i // chunks, i % chunks)

    halo_up().wait_recv()
    halo_down().wait_recv()

    @pl.loop(0, PLANE // step)
    def _(i):
        at = pl.multiple_of(i * step, step)
        for e, plane in enumerate((0, ZDEV + 1)):
            pad[plane, pl.ds(pl.multiple_of(GX + at, GX), step), :] = halo_recv[
                e, pl.ds(at, step), :
            ].astype(F32)

    @pl.loop(0, 2 * chunks)
    def _(i):
        convolve((ZDEV - 1) * (i // chunks), i % chunks)

    @pl.loop(0, heads)
    def _(h):
        send_fwd(h).wait_send()
        send_pair(h).wait_send()
        send_back(h).wait_send()
        send_on(h).wait_send()

    for p in range(2):
        part_copy(p).wait_send()
        stat_copy(p).wait_send()
    halo_up().wait_send()
    halo_down().wait_send()


def on_device(n, tokens, modulation, query_weight, key_weight, value_weight, out_weight, query_gain, key_gain, conv_weight):
    toks, half = tokens.shape
    inner = query_weight.shape[1]
    heads = inner // HD
    vmem = pl.BlockSpec(memory_space=pltpu.VMEM)
    hbm = pl.BlockSpec(memory_space=pl.ANY)
    dma = pltpu.SemaphoreType.DMA
    return pl.pallas_call(
        functools.partial(block_kernel, n),
        out_shape=jax.ShapeDtypeStruct((toks, half), BF16),
        in_specs=[vmem] * 5 + [hbm] * 4,
        out_specs=vmem,
        scratch_shapes=[
            pltpu.VMEM(query_weight.shape, BF16),
            pltpu.VMEM(key_weight.shape, BF16),
            pltpu.VMEM(value_weight.shape, BF16),
            pltpu.VMEM(out_weight.shape, BF16),
            pltpu.VMEM((toks, half), BF16),
            pltpu.VMEM((toks, 2 * half), BF16),
            pltpu.VMEM((5, heads, toks, 2 * HD), BF16),
            pltpu.VMEM((heads, toks, HD), BF16),
            pltpu.VMEM((heads, toks, HD), F32),
            pltpu.VMEM((heads, toks, HD), F32),
            pltpu.VMEM((2, toks // 2, inner), BF16),
            pltpu.VMEM((2, toks // 2, half), BF16),
            pltpu.VMEM((2, toks // 2, half), BF16),
            pltpu.VMEM((2, toks // 2, half), F32),
            pltpu.VMEM((2, toks // 2, HD), F32),
            pltpu.VMEM((2, toks // 2, HD), F32),
            pltpu.VMEM((ZDEV, PLANE, half), F32),
            pltpu.VMEM((ZDEV + 2, PLANE + 2 * GX, half), F32),
            pltpu.VMEM((2, PLANE, half), BF16),
            pltpu.VMEM((2, PLANE, half), BF16),
            pltpu.VMEM((27, half), F32),
            dma((4,)),
            dma((2,)),
            dma((4, heads)),
            dma((4, heads)),
            dma((2, 2)),
            dma((2, 2)),
            dma((2,)),
            dma((2,)),
        ],
        compiler_params=pltpu.CompilerParams(
            collective_id=0, has_side_effects=True, vmem_limit_bytes=52 << 20
        ),
    )(
        tokens,
        modulation,
        query_gain.reshape(1, HD),
        key_gain.reshape(1, HD),
        conv_weight,
        query_weight,
        key_weight,
        value_weight,
        out_weight,
    )


def solution(mesh):
    return jax.shard_map(
        functools.partial(on_device, mesh.shape["seq"]),
        mesh=mesh,
        in_specs=(
            P(("batch", "seq"), "mp"),
            P("batch", None),
            P(None, "mp"),
            P(None, "mp"),
            P(None, "mp"),
            P("mp", None),
            P(),
            P(),
            P(None, "mp"),
        ),
        out_specs=P(("batch", "seq"), "mp"),
        check_vma=False,
    )
```

```python
import functools
import math

import jax
import jax.numpy as jnp
from jax import lax
from jax.experimental import pallas as pl
from jax.experimental.pallas import tpu as pltpu
from jax.sharding import PartitionSpec as P

HD = 128
GX = 16
PLANE = 128
RADIUS = 8
ZDEV = 4
EPS = 1e-06
MESH = pl.DeviceIdType.MESH
F32 = jnp.float32
BF16 = jnp.bfloat16

OWN, PAIR, BELOW, ABOVE, PASSED = range(5)


def block_kernel(
    n,
    x_ref,
    mod_hbm,
    qg_hbm,
    kg_hbm,
    cw_hbm,
    wq_hbm,
    wk_hbm,
    wv_hbm,
    wo_hbm,
    out_ref,
    mod_ref,
    qg_ref,
    kg_ref,
    cw_ref,
    wq,
    wk,
    wv,
    wo,
    x_other,
    x_in,
    x_in_other,
    normed,
    kv,
    qbuf,
    acc,
    den,
    attn,
    part_send,
    part_recv,
    part_own,
    stat_send,
    stat_recv,
    resid,
    pad,
    taps,
    w_sem,
    x_sem,
    kv_send,
    kv_recv,
    xi_send,
    xi_recv,
    xo_send,
    xo_recv,
    part_sem,
    stat_sem,
    halo_ss,
    halo_rs,
):
    toks, half = x_ref.shape
    width = 2 * half
    heads = qbuf.shape[0]
    b = lax.axis_index("batch")
    s = lax.axis_index("seq")
    m = lax.axis_index("mp")
    odd = lax.rem(s, 2)
    pair = s + 1 - 2 * odd
    up1, down1 = lax.rem(s + 1, n), lax.rem(s + n - 1, n)
    up2, down2 = lax.rem(s + 2, n), lax.rem(s + n - 2, n)
    here = pl.multiple_of(m * half, half)
    there = pl.multiple_of((1 - m) * half, half)

    loads = []
    sources = (wk_hbm, wv_hbm, wq_hbm, wo_hbm, mod_hbm, qg_hbm, kg_hbm, cw_hbm)
    targets = (wk, wv, wq, wo, mod_ref, qg_ref, kg_ref, cw_ref)
    for i, (src, dst) in enumerate(zip(sources, targets)):
        load = pltpu.make_async_copy(src, dst, w_sem.at[i])
        load.start()
        loads.append(load)

    peers = [(b, s, 1 - m), (b, up1, m), (b, down1, m), (b, up2, m), (b, down2, m)]
    barrier = pltpu.get_barrier_semaphore()
    for peer in peers:
        pl.semaphore_signal(barrier, inc=1, device_id=peer, device_id_type=MESH)
    pl.semaphore_wait(barrier, len(peers))

    def to(peer, src, dst, send_sem, recv_sem):
        return pltpu.make_async_remote_copy(
            src_ref=src,
            dst_ref=dst,
            send_sem=send_sem,
            recv_sem=recv_sem,
            device_id=peer,
            device_id_type=MESH,
        )

    core = (b, s, 1 - m)
    x_copy = to(core, x_ref, x_other, x_sem.at[0], x_sem.at[1])
    x_copy.start()

    late = pl.ds(PLANE, (ZDEV - 2) * PLANE)

    fwd_slot = ABOVE - odd
    back_slot = BELOW + odd
    fwd_dst = lax.rem(s + n - 2 + 4 * odd, n)
    back_dst = lax.rem(s + 2 + n - 4 * odd, n)

    def send_fwd(h):
        return to((b, fwd_dst, m), kv.at[OWN, h, late], kv.at[fwd_slot, h, late], kv_send.at[0, h], kv_recv.at[0, h])

    def send_pair(h):
        return to((b, pair, m), kv.at[OWN, h, late], kv.at[PAIR, h, late], kv_send.at[1, h], kv_recv.at[1, h])

    def send_back(h):
        return to((b, back_dst, m), kv.at[OWN, h, late], kv.at[back_slot, h, late], kv_send.at[2, h], kv_recv.at[2, h])

    def send_on(h):
        return to((b, pair, m), kv.at[fwd_slot, h, late], kv.at[PASSED, h, late], kv_send.at[3, h], kv_recv.at[3, h])

    def early(e):
        return pl.ds(e * (ZDEV - 1) * PLANE, PLANE)

    def x_to(k, dst, src, slot, e):
        return to((b, dst, m), src, x_in.at[slot - 1, e], xi_send.at[k, e], xi_recv.at[k, e])

    def x_fwd(e):
        return x_to(0, fwd_dst, x_ref.at[early(e)], fwd_slot, e)

    def x_pair(e):
        return x_to(1, pair, x_ref.at[early(e)], PAIR, e)

    def x_back(e):
        return x_to(2, back_dst, x_ref.at[early(e)], back_slot, e)

    def x_on(e):
        return x_to(3, pair, x_in.at[fwd_slot - 1, e], PASSED, e)

    def x_core(k, slot, e):
        return to(core, x_in.at[slot - 1, e], x_in_other.at[slot - 1, e], xo_send.at[k, e], xo_recv.at[k, e])

    for send in (x_fwd, x_pair, x_back):
        for e in range(2):
            send(e).start()

    for load in loads[4:]:
        load.wait()
    pad[:, 0:GX, :] = jnp.zeros((ZDEV + 2, GX, half), F32)
    pad[:, GX + PLANE :, :] = jnp.zeros((ZDEV + 2, GX, half), F32)
    taps[...] = cw_ref[...].astype(F32)
    acc[...] = jnp.zeros_like(acc)
    den[...] = jnp.zeros_like(den)
    x_copy.wait()

    rows_n = 64

    def norm_rows(mine_bf, other_bf, rows):
        mine = mine_bf.astype(F32)
        other = other_bf.astype(F32)
        total = jnp.sum(mine, axis=-1, keepdims=True) + jnp.sum(other, axis=-1, keepdims=True)
        square = jnp.sum(mine * mine, axis=-1, keepdims=True) + jnp.sum(
            other * other, axis=-1, keepdims=True
        )
        mean = total / width
        inv = lax.rsqrt(square / width - mean * mean + EPS)
        for vals, cols in ((mine, pl.ds(here, half)), (other, pl.ds(there, half))):
            normed[rows, cols] = (
                (vals - mean) * inv * (1.0 + mod_ref[1:2, cols]) + mod_ref[0:1, cols]
            ).astype(BF16)

    @pl.loop(0, toks // rows_n)
    def _(i):
        rows = pl.ds(pl.multiple_of(i * rows_n, rows_n), rows_n)
        norm_rows(x_ref[rows, :], x_other[rows, :], rows)

    def head_norm(vals, gain):
        mean_sq = jnp.mean(vals * vals, axis=-1, keepdims=True)
        return vals * lax.rsqrt(mean_sq + EPS) * gain

    loads[0].wait()
    loads[1].wait()

    @pl.loop(0, heads // 2)
    def _(j):
        cols = pl.ds(pl.multiple_of(j * 2 * HD, 2 * HD), 2 * HD)
        keys = jnp.dot(normed[...], wk[:, cols], preferred_element_type=F32)
        for e in range(2):
            kv[OWN, 2 * j + e, :, 0:HD] = head_norm(
                keys[:, e * HD : (e + 1) * HD], kg_ref[...]
            ).astype(BF16)
        values = jnp.dot(normed[...], wv[:, cols], preferred_element_type=F32)
        for e in range(2):
            kv[OWN, 2 * j + e, :, HD:] = values[:, e * HD : (e + 1) * HD].astype(BF16)
        for e in range(2):
            send_fwd(2 * j + e).start()
            send_pair(2 * j + e).start()

    @pl.loop(0, heads)
    def _(h):
        send_back(h).start()

    for e in range(2):
        x_fwd(e).wait_recv()
        x_on(e).start()
        x_core(0, fwd_slot, e).start()
        x_pair(e).wait_recv()
        x_core(1, PAIR, e).start()

    loads[2].wait()

    @pl.loop(0, heads // 2)
    def _(j):
        cols = pl.ds(pl.multiple_of(j * 2 * HD, 2 * HD), 2 * HD)
        queries = jnp.dot(normed[...], wq[:, cols], preferred_element_type=F32)
        for e in range(2):
            qbuf[2 * j + e] = (
                head_norm(queries[:, e * HD : (e + 1) * HD], qg_ref[...]) * HD ** (-0.5)
            ).astype(BF16)

    rows_q = 256

    def attend(slot, h, sign):
        keys = kv[slot, h, :, 0:HD]
        values = kv[slot, h, :, HD:]
        for r in range(toks // rows_q):
            rows = pl.ds(r * rows_q, rows_q)
            scores = lax.dot_general(
                qbuf[h, rows, :], keys, (((1,), (1,)), ((), ())), preferred_element_type=F32
            )
            weights = jnp.exp(scores)
            if sign is not None:
                q_plane = (lax.broadcasted_iota(jnp.int32, scores.shape, 0) + r * rows_q) // PLANE
                k_plane = lax.broadcasted_iota(jnp.int32, scores.shape, 1) // PLANE
                gap = 2 * ZDEV + (k_plane - q_plane) * sign
                weights = jnp.where(gap <= RADIUS, weights, 0.0)
            total = weights[:, 0:HD]
            for c in range(1, toks // HD):
                total = total + weights[:, c * HD : (c + 1) * HD]
            den[h, rows, :] += total
            acc[h, rows, :] += jnp.dot(weights.astype(BF16), values, preferred_element_type=F32)

    @pl.loop(0, heads)
    def _(h):
        attend(OWN, h, None)

    def project(k, slot):
        for e in range(2):
            x_core(k, slot, e).wait_recv()

            @pl.loop(0, PLANE // rows_n)
            def _(i):
                rows = pl.ds(pl.multiple_of(i * rows_n, rows_n), rows_n)
                norm_rows(
                    x_in[slot - 1, e, rows, :],
                    x_in_other[slot - 1, e, rows, :],
                    pl.ds(pl.multiple_of(e * PLANE + i * rows_n, rows_n), rows_n),
                )

        @pl.loop(0, heads // 2)
        def _(j):
            cols = pl.ds(pl.multiple_of(j * 2 * HD, 2 * HD), 2 * HD)
            keys = jnp.dot(normed[0 : 2 * PLANE, :], wk[:, cols], preferred_element_type=F32)
            values = jnp.dot(normed[0 : 2 * PLANE, :], wv[:, cols], preferred_element_type=F32)
            for d in range(2):
                key_d = head_norm(keys[:, d * HD : (d + 1) * HD], kg_ref[...]).astype(BF16)
                value_d = values[:, d * HD : (d + 1) * HD].astype(BF16)
                for e in range(2):
                    part = slice(e * PLANE, (e + 1) * PLANE)
                    kv[slot, 2 * j + d, early(e), 0:HD] = key_d[part]
                    kv[slot, 2 * j + d, early(e), HD:] = value_d[part]

    project(0, fwd_slot)
    project(1, PAIR)
    for e in range(2):
        x_back(e).wait_recv()
        x_core(2, back_slot, e).start()
    project(2, back_slot)
    for e in range(2):
        x_on(e).wait_recv()
        x_core(3, PASSED, e).start()
    project(3, PASSED)

    @pl.loop(0, heads)
    def _(h):
        send_fwd(h).wait_recv()
        send_on(h).start()
        send_pair(h).wait_recv()
        attend(PAIR, h, None)
        attend(fwd_slot, h, 1 - 2 * odd)

    @pl.loop(0, heads)
    def _(h):
        send_back(h).wait_recv()
        attend(back_slot, h, 2 * odd - 1)

    planes_of = ((0, ZDEV - 1), (1, 2))

    @pl.loop(0, heads)
    def _(h):
        send_on(h).wait_recv()
        attend(PASSED, h, None)
        cols = pl.ds(pl.multiple_of(h * HD, HD), HD)
        for p, planes in enumerate(planes_of):
            for e, plane in enumerate(planes):
                rows = pl.ds(plane * PLANE, PLANE)
                total = jnp.sum(den[h, rows, :], axis=-1, keepdims=True)
                attn[p, e * PLANE : (e + 1) * PLANE, cols] = (acc[h, rows, :] / total).astype(BF16)

    loads[3].wait()
    tile = 256

    def part_copy(p):
        return to(core, part_send.at[p], part_recv.at[p], part_sem.at[0, p], part_sem.at[1, p])

    def stat_copy(p):
        return to(core, stat_send.at[p], stat_recv.at[p], stat_sem.at[0, p], stat_sem.at[1, p])

    def halo_up():
        return to(
            (b, up1, m),
            attn.at[0, pl.ds(PLANE, PLANE)],
            attn.at[2, pl.ds(0, PLANE)],
            halo_ss.at[0],
            halo_rs.at[0],
        )

    def halo_down():
        return to(
            (b, down1, m),
            attn.at[0, pl.ds(0, PLANE)],
            attn.at[2, pl.ds(PLANE, PLANE)],
            halo_ss.at[1],
            halo_rs.at[1],
        )

    halo_up().start()
    halo_down().start()
    mine = pl.ds(here, half)
    step = 32

    def part(p):
        @pl.loop(0, half // tile)
        def _(c):
            at = pl.multiple_of(c * tile, tile)
            src = pl.ds(pl.multiple_of(there + at, tile), tile)
            part_send[p, :, pl.ds(at, tile)] = jnp.dot(
                attn[p], wo[:, src], preferred_element_type=F32
            ).astype(BF16)

        part_copy(p).start()

    def own(p):
        @pl.loop(0, half // tile)
        def _(c):
            at = pl.multiple_of(c * tile, tile)
            src = pl.ds(pl.multiple_of(here + at, tile), tile)
            part_own[p, :, pl.ds(at, tile)] = jnp.dot(attn[p], wo[:, src], preferred_element_type=F32)

    halo_slots = (3 - 3 * odd, 3 * odd)

    def residual(p):
        part_copy(p).wait_recv()
        for e in range(2):

            @pl.loop(0, PLANE // step)
            def _(i):
                at = pl.multiple_of(i * step, step)
                local = pl.ds(pl.multiple_of(e * PLANE + at, step), step)
                attended = part_own[p, local, :] + part_recv[p, local, :].astype(F32)
                if p < 2:
                    plane = planes_of[p][e]
                    base = x_ref[pl.ds(pl.multiple_of(plane * PLANE + at, step), step), :]
                else:
                    plane = ZDEV + e
                    base = x_in[halo_slots[e], 1 - e, pl.ds(at, step), :]
                vals = base.astype(F32) + mod_ref[2:3, mine] * attended
                resid[plane, pl.ds(at, step), :] = vals
                lane = lax.broadcasted_iota(jnp.int32, (step, HD), 1)
                stat_send[p, local, :] = jnp.where(
                    lane < HD // 2,
                    jnp.sum(vals, axis=-1, keepdims=True),
                    jnp.sum(vals * vals, axis=-1, keepdims=True),
                )

        stat_copy(p).start()

    def shape(p):
        stat_copy(p).wait_recv()
        for e in range(2):

            @pl.loop(0, PLANE // step)
            def _(i):
                at = pl.multiple_of(i * step, step)
                local = pl.ds(pl.multiple_of(e * PLANE + at, step), step)
                stats = stat_send[p, local, :] + stat_recv[p, local, :]
                center = stats[:, 0:1] / width
                spread = stats[:, HD // 2 : HD // 2 + 1] / width - center * center
                plane = planes_of[p][e] if p < 2 else ZDEV + e
                slab = plane + 1 if p < 2 else e * (ZDEV + 1)
                shaped = (
                    (resid[plane, pl.ds(at, step), :] - center)
                    * lax.rsqrt(spread + EPS)
                    * (1.0 + mod_ref[4:5, mine])
                    + mod_ref[3:4, mine]
                ).astype(BF16)
                pad[slab, pl.ds(pl.multiple_of(GX + at, GX), step), :] = shaped.astype(F32)

    part(0)
    part(1)
    own(0)
    own(1)
    residual(0)
    residual(1)
    halo_up().wait_recv()
    halo_down().wait_recv()
    part(2)
    own(2)
    shape(0)
    shape(1)
    residual(2)

    rows_c = 64

    def convolve(plane, lc):
        lane_at = pl.multiple_of(lc * HD, HD)
        lanes = pl.ds(lane_at, HD)
        gate = mod_ref[5:6, pl.ds(pl.multiple_of(here + lane_at, HD), HD)]
        col = lax.rem(lax.broadcasted_iota(jnp.int32, (rows_c, HD), 0), GX)
        for r in range(PLANE // rows_c):
            sums = [None] * 3
            for dz in range(3):
                for dy in range(3):
                    window = pad[plane + dz, pl.ds(r * rows_c + GX * dy, rows_c), lanes]
                    for dx in range(3):
                        k = (dz * 3 + dy) * 3 + dx
                        term = window * taps[k : k + 1, lanes]
                        sums[dx] = term if sums[dx] is None else sums[dx] + term
            v = (
                sums[1]
                + jnp.where(col > 0, pltpu.roll(sums[0], 1, 0), 0.0)
                + jnp.where(col < GX - 1, pltpu.roll(sums[2], rows_c - 1, 0), 0.0)
            )
            gelu = 0.5 * v * (1.0 + jnp.tanh(math.sqrt(2.0 / math.pi) * (v + 0.044715 * (v * v * v))))
            result = resid[plane, pl.ds(r * rows_c, rows_c), lanes] + gate * gelu
            at = pl.multiple_of(plane * PLANE + r * rows_c, rows_c)
            out_ref[pl.ds(at, rows_c), lanes] = result.astype(BF16)

    chunks = half // HD

    @pl.loop(0, 2 * chunks)
    def _(i):
        convolve(1 + i // chunks, i % chunks)

    shape(2)

    @pl.loop(0, 2 * chunks)
    def _(i):
        convolve((ZDEV - 1) * (i // chunks), i % chunks)

    @pl.loop(0, heads)
    def _(h):
        send_fwd(h).wait_send()
        send_pair(h).wait_send()
        send_back(h).wait_send()
        send_on(h).wait_send()

    for e in range(2):
        x_fwd(e).wait_send()
        x_pair(e).wait_send()
        x_back(e).wait_send()
        x_on(e).wait_send()
        for k, slot in enumerate((fwd_slot, PAIR, back_slot, PASSED)):
            x_core(k, slot, e).wait_send()
    for p in range(3):
        part_copy(p).wait_send()
        stat_copy(p).wait_send()
    halo_up().wait_send()
    halo_down().wait_send()


def on_device(n, tokens, modulation, query_weight, key_weight, value_weight, out_weight, query_gain, key_gain, conv_weight):
    toks, half = tokens.shape
    inner = query_weight.shape[1]
    heads = inner // HD
    vmem = pl.BlockSpec(memory_space=pltpu.VMEM)
    hbm = pl.BlockSpec(memory_space=pltpu.HBM)
    dma = pltpu.SemaphoreType.DMA
    return pl.pallas_call(
        functools.partial(block_kernel, n),
        out_shape=jax.ShapeDtypeStruct((toks, half), BF16),
        in_specs=[vmem] + [hbm] * 8,
        out_specs=vmem,
        scratch_shapes=[
            pltpu.VMEM(modulation.shape, F32),
            pltpu.VMEM((1, HD), F32),
            pltpu.VMEM((1, HD), F32),
            pltpu.VMEM(conv_weight.shape, BF16),
            pltpu.VMEM(query_weight.shape, BF16),
            pltpu.VMEM(key_weight.shape, BF16),
            pltpu.VMEM(value_weight.shape, BF16),
            pltpu.VMEM(out_weight.shape, BF16),
            pltpu.VMEM((toks, half), BF16),
            pltpu.VMEM((4, 2, PLANE, half), BF16),
            pltpu.VMEM((4, 2, PLANE, half), BF16),
            pltpu.VMEM((toks, 2 * half), BF16),
            pltpu.VMEM((5, heads, toks, 2 * HD), BF16),
            pltpu.VMEM((heads, toks, HD), BF16),
            pltpu.VMEM((heads, toks, HD), F32),
            pltpu.VMEM((heads, toks, HD), F32),
            pltpu.VMEM((3, 2 * PLANE, inner), BF16),
            pltpu.VMEM((3, 2 * PLANE, half), BF16),
            pltpu.VMEM((3, 2 * PLANE, half), BF16),
            pltpu.VMEM((3, 2 * PLANE, half), F32),
            pltpu.VMEM((3, 2 * PLANE, HD), F32),
            pltpu.VMEM((3, 2 * PLANE, HD), F32),
            pltpu.VMEM((ZDEV + 2, PLANE, half), F32),
            pltpu.VMEM((ZDEV + 2, PLANE + 2 * GX, half), F32),
            pltpu.VMEM((27, half), F32),
            dma((8,)),
            dma((2,)),
            dma((4, heads)),
            dma((4, heads)),
            dma((4, 2)),
            dma((4, 2)),
            dma((4, 2)),
            dma((4, 2)),
            dma((2, 3)),
            dma((2, 3)),
            dma((2,)),
            dma((2,)),
        ],
        compiler_params=pltpu.CompilerParams(
            collective_id=0, has_side_effects=True, vmem_limit_bytes=60 << 20
        ),
    )(
        tokens,
        modulation,
        query_gain.reshape(1, HD),
        key_gain.reshape(1, HD),
        conv_weight,
        query_weight,
        key_weight,
        value_weight,
        out_weight,
    )


def solution(mesh):
    return jax.shard_map(
        functools.partial(on_device, mesh.shape["seq"]),
        mesh=mesh,
        in_specs=(
            P(("batch", "seq"), "mp"),
            P("batch", None),
            P(None, "mp"),
            P(None, "mp"),
            P(None, "mp"),
            P("mp", None),
            P(),
            P(),
            P(None, "mp"),
        ),
        out_specs=P(("batch", "seq"), "mp"),
        check_vma=False,
    )
```

```python
import functools
import math

import jax
import jax.numpy as jnp
from jax import lax
from jax.experimental import pallas as pl
from jax.experimental.pallas import tpu as pltpu
from jax.sharding import PartitionSpec as P

HD = 128
GX = 16
PLANE = 128
RADIUS = 8
ZDEV = 4
EPS = 1e-06
MESH = pl.DeviceIdType.MESH
F32 = jnp.float32
BF16 = jnp.bfloat16

OWN, PAIR, BELOW, ABOVE, PASSED = range(5)


def block_kernel(
    n,
    x_ref,
    mod_hbm,
    qg_hbm,
    kg_hbm,
    cw_hbm,
    wq_hbm,
    wk_hbm,
    wv_hbm,
    wo_hbm,
    out_ref,
    mod_ref,
    qg_ref,
    kg_ref,
    cw_ref,
    wq,
    wk,
    wv,
    wo,
    x_other,
    x_in,
    x_in_other,
    normed,
    kv,
    qbuf,
    acc,
    den,
    attn,
    part_send,
    part_recv,
    part_own,
    stat_send,
    stat_recv,
    resid,
    pad,
    taps,
    w_sem,
    x_sem,
    kv_send,
    kv_recv,
    xi_send,
    xi_recv,
    xo_send,
    xo_recv,
    part_sem,
    stat_sem,
    halo_ss,
    halo_rs,
):
    toks, half = x_ref.shape
    width = 2 * half
    heads = qbuf.shape[0]
    b = lax.axis_index("batch")
    s = lax.axis_index("seq")
    m = lax.axis_index("mp")
    odd = lax.rem(s, 2)
    pair = s + 1 - 2 * odd
    up1, down1 = lax.rem(s + 1, n), lax.rem(s + n - 1, n)
    up2, down2 = lax.rem(s + 2, n), lax.rem(s + n - 2, n)
    here = pl.multiple_of(m * half, half)
    there = pl.multiple_of((1 - m) * half, half)

    loads = []
    sources = (wk_hbm, wv_hbm, wq_hbm, wo_hbm, mod_hbm, qg_hbm, kg_hbm, cw_hbm)
    targets = (wk, wv, wq, wo, mod_ref, qg_ref, kg_ref, cw_ref)
    for i, (src, dst) in enumerate(zip(sources, targets)):
        load = pltpu.make_async_copy(src, dst, w_sem.at[i])
        load.start()
        loads.append(load)

    peers = [(b, s, 1 - m), (b, up1, m), (b, down1, m), (b, up2, m), (b, down2, m)]
    barrier = pltpu.get_barrier_semaphore()
    for peer in peers:
        pl.semaphore_signal(barrier, inc=1, device_id=peer, device_id_type=MESH)
    pl.semaphore_wait(barrier, len(peers))

    def to(peer, src, dst, send_sem, recv_sem):
        return pltpu.make_async_remote_copy(
            src_ref=src,
            dst_ref=dst,
            send_sem=send_sem,
            recv_sem=recv_sem,
            device_id=peer,
            device_id_type=MESH,
        )

    core = (b, s, 1 - m)
    x_copy = to(core, x_ref, x_other, x_sem.at[0], x_sem.at[1])
    x_copy.start()

    late = pl.ds(PLANE, (ZDEV - 2) * PLANE)

    fwd_slot = ABOVE - odd
    back_slot = BELOW + odd
    fwd_dst = lax.rem(s + n - 2 + 4 * odd, n)
    back_dst = lax.rem(s + 2 + n - 4 * odd, n)

    def send_fwd(h):
        return to((b, fwd_dst, m), kv.at[OWN, h, late], kv.at[fwd_slot, h, late], kv_send.at[0, h], kv_recv.at[0, h])

    def send_pair(h):
        return to((b, pair, m), kv.at[OWN, h, late], kv.at[PAIR, h, late], kv_send.at[1, h], kv_recv.at[1, h])

    def send_back(h):
        return to((b, back_dst, m), kv.at[OWN, h, late], kv.at[back_slot, h, late], kv_send.at[2, h], kv_recv.at[2, h])

    def send_on(h):
        return to((b, pair, m), kv.at[fwd_slot, h, late], kv.at[PASSED, h, late], kv_send.at[3, h], kv_recv.at[3, h])

    def early(e):
        return pl.ds(e * (ZDEV - 1) * PLANE, PLANE)

    def x_to(k, dst, src, slot, e):
        return to((b, dst, m), src, x_in.at[slot - 1, e], xi_send.at[k, e], xi_recv.at[k, e])

    def x_fwd(e):
        return x_to(0, fwd_dst, x_ref.at[early(e)], fwd_slot, e)

    def x_pair(e):
        return x_to(1, pair, x_ref.at[early(e)], PAIR, e)

    def x_back(e):
        return x_to(2, back_dst, x_ref.at[early(e)], back_slot, e)

    def x_on(e):
        return x_to(3, pair, x_in.at[fwd_slot - 1, e], PASSED, e)

    def x_core(k, slot, e):
        return to(core, x_in.at[slot - 1, e], x_in_other.at[slot - 1, e], xo_send.at[k, e], xo_recv.at[k, e])

    for send in (x_fwd, x_pair, x_back):
        for e in range(2):
            send(e).start()

    for load in loads[4:]:
        load.wait()
    pad[:, 0:GX, :] = jnp.zeros((ZDEV + 2, GX, half), F32)
    pad[:, GX + PLANE :, :] = jnp.zeros((ZDEV + 2, GX, half), F32)
    taps[...] = cw_ref[...].astype(F32)
    acc[...] = jnp.zeros_like(acc)
    den[...] = jnp.zeros_like(den)
    x_copy.wait()

    rows_n = 64

    def norm_rows(mine_bf, other_bf, rows):
        mine = mine_bf.astype(F32)
        other = other_bf.astype(F32)
        total = jnp.sum(mine, axis=-1, keepdims=True) + jnp.sum(other, axis=-1, keepdims=True)
        square = jnp.sum(mine * mine, axis=-1, keepdims=True) + jnp.sum(
            other * other, axis=-1, keepdims=True
        )
        mean = total / width
        inv = lax.rsqrt(square / width - mean * mean + EPS)
        for vals, cols in ((mine, pl.ds(here, half)), (other, pl.ds(there, half))):
            normed[rows, cols] = (
                (vals - mean) * inv * (1.0 + mod_ref[1:2, cols]) + mod_ref[0:1, cols]
            ).astype(BF16)

    @pl.loop(0, toks // rows_n)
    def _(i):
        rows = pl.ds(pl.multiple_of(i * rows_n, rows_n), rows_n)
        norm_rows(x_ref[rows, :], x_other[rows, :], rows)

    def head_norm(vals, gain):
        mean_sq = jnp.mean(vals * vals, axis=-1, keepdims=True)
        return vals * lax.rsqrt(mean_sq + EPS) * gain

    loads[0].wait()
    loads[1].wait()

    @pl.loop(0, heads // 2)
    def _(j):
        cols = pl.ds(pl.multiple_of(j * 2 * HD, 2 * HD), 2 * HD)
        keys = jnp.dot(normed[...], wk[:, cols], preferred_element_type=F32)
        for e in range(2):
            kv[OWN, 2 * j + e, :, 0:HD] = head_norm(
                keys[:, e * HD : (e + 1) * HD], kg_ref[...]
            ).astype(BF16)
        values = jnp.dot(normed[...], wv[:, cols], preferred_element_type=F32)
        for e in range(2):
            kv[OWN, 2 * j + e, :, HD:] = values[:, e * HD : (e + 1) * HD].astype(BF16)
        for e in range(2):
            send_fwd(2 * j + e).start()
            send_pair(2 * j + e).start()

    @pl.loop(0, heads)
    def _(h):
        send_back(h).start()

    for e in range(2):
        x_fwd(e).wait_recv()
        x_on(e).start()
        x_core(0, fwd_slot, e).start()
        x_pair(e).wait_recv()
        x_core(1, PAIR, e).start()

    loads[2].wait()

    @pl.loop(0, heads // 2)
    def _(j):
        cols = pl.ds(pl.multiple_of(j * 2 * HD, 2 * HD), 2 * HD)
        queries = jnp.dot(normed[...], wq[:, cols], preferred_element_type=F32)
        for e in range(2):
            qbuf[2 * j + e] = (
                head_norm(queries[:, e * HD : (e + 1) * HD], qg_ref[...]) * HD ** (-0.5)
            ).astype(BF16)

    rows_q = 256

    def attend(slot, h, sign):
        keys = kv[slot, h, :, 0:HD]
        values = kv[slot, h, :, HD:]
        for r in range(toks // rows_q):
            rows = pl.ds(r * rows_q, rows_q)
            scores = lax.dot_general(
                qbuf[h, rows, :], keys, (((1,), (1,)), ((), ())), preferred_element_type=F32
            )
            weights = jnp.exp(scores)
            if sign is not None:
                q_plane = (lax.broadcasted_iota(jnp.int32, scores.shape, 0) + r * rows_q) // PLANE
                k_plane = lax.broadcasted_iota(jnp.int32, scores.shape, 1) // PLANE
                gap = 2 * ZDEV + (k_plane - q_plane) * sign
                weights = jnp.where(gap <= RADIUS, weights, 0.0)
            total = weights[:, 0:HD]
            for c in range(1, toks // HD):
                total = total + weights[:, c * HD : (c + 1) * HD]
            den[h, rows, :] += total
            acc[h, rows, :] += jnp.dot(weights.astype(BF16), values, preferred_element_type=F32)

    @pl.loop(0, heads)
    def _(h):
        attend(OWN, h, None)

    def project(k, slot):
        for e in range(2):
            x_core(k, slot, e).wait_recv()

            @pl.loop(0, PLANE // rows_n)
            def _(i):
                rows = pl.ds(pl.multiple_of(i * rows_n, rows_n), rows_n)
                norm_rows(
                    x_in[slot - 1, e, rows, :],
                    x_in_other[slot - 1, e, rows, :],
                    pl.ds(pl.multiple_of(e * PLANE + i * rows_n, rows_n), rows_n),
                )

        @pl.loop(0, heads // 2)
        def _(j):
            cols = pl.ds(pl.multiple_of(j * 2 * HD, 2 * HD), 2 * HD)
            keys = jnp.dot(normed[0 : 2 * PLANE, :], wk[:, cols], preferred_element_type=F32)
            values = jnp.dot(normed[0 : 2 * PLANE, :], wv[:, cols], preferred_element_type=F32)
            for d in range(2):
                key_d = head_norm(keys[:, d * HD : (d + 1) * HD], kg_ref[...]).astype(BF16)
                value_d = values[:, d * HD : (d + 1) * HD].astype(BF16)
                for e in range(2):
                    part = slice(e * PLANE, (e + 1) * PLANE)
                    kv[slot, 2 * j + d, early(e), 0:HD] = key_d[part]
                    kv[slot, 2 * j + d, early(e), HD:] = value_d[part]

    project(0, fwd_slot)
    project(1, PAIR)
    for e in range(2):
        x_back(e).wait_recv()
        x_core(2, back_slot, e).start()
    project(2, back_slot)
    for e in range(2):
        x_on(e).wait_recv()
        x_core(3, PASSED, e).start()
    project(3, PASSED)

    @pl.loop(0, heads)
    def _(h):
        send_fwd(h).wait_recv()
        send_on(h).start()
        send_pair(h).wait_recv()
        attend(PAIR, h, None)
        attend(fwd_slot, h, 1 - 2 * odd)

    @pl.loop(0, heads)
    def _(h):
        send_back(h).wait_recv()
        attend(back_slot, h, 2 * odd - 1)

    def head_cols(h):
        return pl.ds(pl.multiple_of(h * HD, HD), HD)

    def halo_up(h):
        return to(
            (b, up1, m),
            attn.at[0, pl.ds(PLANE, PLANE), head_cols(h)],
            attn.at[2, pl.ds(0, PLANE), head_cols(h)],
            halo_ss.at[0, h],
            halo_rs.at[0, h],
        )

    def halo_down(h):
        return to(
            (b, down1, m),
            attn.at[0, pl.ds(0, PLANE), head_cols(h)],
            attn.at[2, pl.ds(PLANE, PLANE), head_cols(h)],
            halo_ss.at[1, h],
            halo_rs.at[1, h],
        )

    planes_of = ((0, ZDEV - 1), (1, 2))

    @pl.loop(0, heads)
    def _(h):
        send_on(h).wait_recv()
        attend(PASSED, h, None)
        cols = pl.ds(pl.multiple_of(h * HD, HD), HD)
        for p, planes in enumerate(planes_of):
            for e, plane in enumerate(planes):
                rows = pl.ds(plane * PLANE, PLANE)
                total = jnp.sum(den[h, rows, :], axis=-1, keepdims=True)
                attn[p, e * PLANE : (e + 1) * PLANE, cols] = (acc[h, rows, :] / total).astype(BF16)
        halo_up(h).start()
        halo_down(h).start()

    loads[3].wait()
    tile = 256

    def part_copy(p):
        return to(core, part_send.at[p], part_recv.at[p], part_sem.at[0, p], part_sem.at[1, p])

    def stat_copy(p):
        return to(core, stat_send.at[p], stat_recv.at[p], stat_sem.at[0, p], stat_sem.at[1, p])

    mine = pl.ds(here, half)
    step = 32

    def part(p):
        @pl.loop(0, half // tile)
        def _(c):
            at = pl.multiple_of(c * tile, tile)
            src = pl.ds(pl.multiple_of(there + at, tile), tile)
            part_send[p, :, pl.ds(at, tile)] = jnp.dot(
                attn[p], wo[:, src], preferred_element_type=F32
            ).astype(BF16)

        part_copy(p).start()

    def own(p):
        @pl.loop(0, half // tile)
        def _(c):
            at = pl.multiple_of(c * tile, tile)
            src = pl.ds(pl.multiple_of(here + at, tile), tile)
            part_own[p, :, pl.ds(at, tile)] = jnp.dot(attn[p], wo[:, src], preferred_element_type=F32)

    halo_slots = (3 - 3 * odd, 3 * odd)

    def residual(p):
        part_copy(p).wait_recv()
        for e in range(2):

            @pl.loop(0, PLANE // step)
            def _(i):
                at = pl.multiple_of(i * step, step)
                local = pl.ds(pl.multiple_of(e * PLANE + at, step), step)
                attended = part_own[p, local, :] + part_recv[p, local, :].astype(F32)
                if p < 2:
                    plane = planes_of[p][e]
                    base = x_ref[pl.ds(pl.multiple_of(plane * PLANE + at, step), step), :]
                else:
                    plane = ZDEV + e
                    base = x_in[halo_slots[e], 1 - e, pl.ds(at, step), :]
                vals = base.astype(F32) + mod_ref[2:3, mine] * attended
                resid[plane, pl.ds(at, step), :] = vals
                lane = lax.broadcasted_iota(jnp.int32, (step, HD), 1)
                stat_send[p, local, :] = jnp.where(
                    lane < HD // 2,
                    jnp.sum(vals, axis=-1, keepdims=True),
                    jnp.sum(vals * vals, axis=-1, keepdims=True),
                )

        stat_copy(p).start()

    def shape(p):
        stat_copy(p).wait_recv()
        for e in range(2):

            @pl.loop(0, PLANE // step)
            def _(i):
                at = pl.multiple_of(i * step, step)
                local = pl.ds(pl.multiple_of(e * PLANE + at, step), step)
                stats = stat_send[p, local, :] + stat_recv[p, local, :]
                center = stats[:, 0:1] / width
                spread = stats[:, HD // 2 : HD // 2 + 1] / width - center * center
                plane = planes_of[p][e] if p < 2 else ZDEV + e
                slab = plane + 1 if p < 2 else e * (ZDEV + 1)
                shaped = (
                    (resid[plane, pl.ds(at, step), :] - center)
                    * lax.rsqrt(spread + EPS)
                    * (1.0 + mod_ref[4:5, mine])
                    + mod_ref[3:4, mine]
                ).astype(BF16)
                pad[slab, pl.ds(pl.multiple_of(GX + at, GX), step), :] = shaped.astype(F32)

    part(0)
    part(1)
    own(0)
    own(1)
    residual(0)
    residual(1)

    @pl.loop(0, heads)
    def _(h):
        halo_up(h).wait_recv()
        halo_down(h).wait_recv()

    part(2)
    own(2)
    shape(0)
    shape(1)
    residual(2)

    rows_c = 64

    def convolve(plane, lc):
        lane_at = pl.multiple_of(lc * HD, HD)
        lanes = pl.ds(lane_at, HD)
        gate = mod_ref[5:6, pl.ds(pl.multiple_of(here + lane_at, HD), HD)]
        col = lax.rem(lax.broadcasted_iota(jnp.int32, (rows_c, HD), 0), GX)
        for r in range(PLANE // rows_c):
            sums = [None] * 3
            for dz in range(3):
                for dy in range(3):
                    window = pad[plane + dz, pl.ds(r * rows_c + GX * dy, rows_c), lanes]
                    for dx in range(3):
                        k = (dz * 3 + dy) * 3 + dx
                        term = window * taps[k : k + 1, lanes]
                        sums[dx] = term if sums[dx] is None else sums[dx] + term
            v = (
                sums[1]
                + jnp.where(col > 0, pltpu.roll(sums[0], 1, 0), 0.0)
                + jnp.where(col < GX - 1, pltpu.roll(sums[2], rows_c - 1, 0), 0.0)
            )
            gelu = 0.5 * v * (1.0 + jnp.tanh(math.sqrt(2.0 / math.pi) * (v + 0.044715 * (v * v * v))))
            result = resid[plane, pl.ds(r * rows_c, rows_c), lanes] + gate * gelu
            at = pl.multiple_of(plane * PLANE + r * rows_c, rows_c)
            out_ref[pl.ds(at, rows_c), lanes] = result.astype(BF16)

    chunks = half // HD

    @pl.loop(0, 2 * chunks)
    def _(i):
        convolve(1 + i // chunks, i % chunks)

    shape(2)

    @pl.loop(0, 2 * chunks)
    def _(i):
        convolve((ZDEV - 1) * (i // chunks), i % chunks)

    @pl.loop(0, heads)
    def _(h):
        send_fwd(h).wait_send()
        send_pair(h).wait_send()
        send_back(h).wait_send()
        send_on(h).wait_send()

    for e in range(2):
        x_fwd(e).wait_send()
        x_pair(e).wait_send()
        x_back(e).wait_send()
        x_on(e).wait_send()
        for k, slot in enumerate((fwd_slot, PAIR, back_slot, PASSED)):
            x_core(k, slot, e).wait_send()
    for p in range(3):
        part_copy(p).wait_send()
        stat_copy(p).wait_send()

    @pl.loop(0, heads)
    def _(h):
        halo_up(h).wait_send()
        halo_down(h).wait_send()


def on_device(n, tokens, modulation, query_weight, key_weight, value_weight, out_weight, query_gain, key_gain, conv_weight):
    toks, half = tokens.shape
    inner = query_weight.shape[1]
    heads = inner // HD
    vmem = pl.BlockSpec(memory_space=pltpu.VMEM)
    hbm = pl.BlockSpec(memory_space=pltpu.HBM)
    dma = pltpu.SemaphoreType.DMA
    return pl.pallas_call(
        functools.partial(block_kernel, n),
        out_shape=jax.ShapeDtypeStruct((toks, half), BF16),
        in_specs=[vmem] + [hbm] * 8,
        out_specs=vmem,
        scratch_shapes=[
            pltpu.VMEM(modulation.shape, F32),
            pltpu.VMEM((1, HD), F32),
            pltpu.VMEM((1, HD), F32),
            pltpu.VMEM(conv_weight.shape, BF16),
            pltpu.VMEM(query_weight.shape, BF16),
            pltpu.VMEM(key_weight.shape, BF16),
            pltpu.VMEM(value_weight.shape, BF16),
            pltpu.VMEM(out_weight.shape, BF16),
            pltpu.VMEM((toks, half), BF16),
            pltpu.VMEM((4, 2, PLANE, half), BF16),
            pltpu.VMEM((4, 2, PLANE, half), BF16),
            pltpu.VMEM((toks, 2 * half), BF16),
            pltpu.VMEM((5, heads, toks, 2 * HD), BF16),
            pltpu.VMEM((heads, toks, HD), BF16),
            pltpu.VMEM((heads, toks, HD), F32),
            pltpu.VMEM((heads, toks, HD), F32),
            pltpu.VMEM((3, 2 * PLANE, inner), BF16),
            pltpu.VMEM((3, 2 * PLANE, half), BF16),
            pltpu.VMEM((3, 2 * PLANE, half), BF16),
            pltpu.VMEM((3, 2 * PLANE, half), F32),
            pltpu.VMEM((3, 2 * PLANE, HD), F32),
            pltpu.VMEM((3, 2 * PLANE, HD), F32),
            pltpu.VMEM((ZDEV + 2, PLANE, half), F32),
            pltpu.VMEM((ZDEV + 2, PLANE + 2 * GX, half), F32),
            pltpu.VMEM((27, half), F32),
            dma((8,)),
            dma((2,)),
            dma((4, heads)),
            dma((4, heads)),
            dma((4, 2)),
            dma((4, 2)),
            dma((4, 2)),
            dma((4, 2)),
            dma((2, 3)),
            dma((2, 3)),
            dma((2, heads)),
            dma((2, heads)),
        ],
        compiler_params=pltpu.CompilerParams(
            collective_id=0, has_side_effects=True, vmem_limit_bytes=60 << 20
        ),
    )(
        tokens,
        modulation,
        query_gain.reshape(1, HD),
        key_gain.reshape(1, HD),
        conv_weight,
        query_weight,
        key_weight,
        value_weight,
        out_weight,
    )


def solution(mesh):
    return jax.shard_map(
        functools.partial(on_device, mesh.shape["seq"]),
        mesh=mesh,
        in_specs=(
            P(("batch", "seq"), "mp"),
            P("batch", None),
            P(None, "mp"),
            P(None, "mp"),
            P(None, "mp"),
            P("mp", None),
            P(),
            P(),
            P(None, "mp"),
        ),
        out_specs=P(("batch", "seq"), "mp"),
        check_vma=False,
    )
```
